32 devices in a mesh: dom: 16 (over z, y, x), head: 2 (over core).
Axes of the slice: x: 2, y: 2, z: 4, core: 2. Of those that a mesh axis runs over, the one named last changes fastest.
Arguments:
- query_rows: bfloat16 [4096, 512], P('dom', 'head'), may hold values from -70 to 70
- key_rows: bfloat16 [4096, 512], P('dom', 'head'), may hold values from -4 to 4
- value_rows: bfloat16 [4096, 512], P('dom', 'head'), may hold values from -6 to 6
- out_weight: bfloat16 [512, 512], P('head'), may hold values from -0.25 to 0.25
- out_grad: bfloat16 [4096, 512], P('dom', 'head'), may hold values from -6 to 6
- far_bias: float32 [8], P('head'), may hold values from 4 to 7
- tile_list: int32 [32, 4], P('dom'), may hold values from 0 to 31, as said below
- tile_count: int32 [32], P('dom'), may hold values from 1 to 4, as said below
- send_rows: int32 [16, 16, 64], P('dom'), may hold values from 0 to 255
- expander_slot: int32 [4096, 3], P('dom'), may hold values from 0 to 1023, as said below
Outputs:
- layer_out: bfloat16 [4096, 512], P('dom', 'head')
- query_grad: bfloat16 [4096, 512], P('dom', 'head')
- key_grad: bfloat16 [4096, 512], P('dom', 'head')
- value_grad: bfloat16 [4096, 512], P('dom', 'head')
- out_weight_grad: float32 [512, 512], P('dom', 'head')
The draws below stay inside these ranges and needn't reach their ends.
Inputs may be any that keep to these rules, and one draw needn't show every extreme that they name: `tile_list`: row t begins with t itself; its first tile_count[t] entries are distinct tiles from the 2 last tiles of the previous partition, the 2 tiles of t's own partition and the 2 first tiles of the next partition (partition = block of 2 tiles); later entries equal t. `tile_count`: every partition of 2 tiles has a tile with 4. `expander_slot`: A value names source partition value // 64 and slot value % 64 of send_rows[source, partition of the node].
All inputs are finite; a program needn't handle non-finite values.
Results may differ from the reference program's by a relative error of at most 0.011.
Values may be sent and summed in bfloat16 or wider, within the bound.
A program may use at most 64 MiB of HBM per device.

```python
import jax
import jax.numpy as jnp
from jax import lax

D = 512
HEADS = 8
TILE = 128
NODE_DEV = 256
KT = 4
HALO = 2
DEG = 3
NODES = 4096
TILES = 32
TPD = 2
CAP = 64
N_DOM = 16


def query_key_pair(seed_key):
    base_key = jax.random.fold_in(seed_key, 7)
    query_key, keys_key = jax.random.split(base_key, 2)
    shape_pair = (NODES, D)
    query_draw = jnp.clip(jax.random.normal(query_key, shape_pair, jnp.float32), -4.0, 4.0)
    key_draw = jnp.clip(jax.random.normal(keys_key, shape_pair, jnp.float32), -4.0, 4.0)
    return (query_draw, key_draw)


def draw_query_rows(key, part):
    return query_key_pair(key)[0].astype(jnp.bfloat16)


def draw_key_rows(key, part):
    return query_key_pair(key)[1].astype(jnp.bfloat16)


def tile_plan(seed_key):
    base_key = jax.random.fold_in(seed_key, 3)
    pick_key, low_key, spread_key, force_key = jax.random.split(base_key, 4)
    cand_width = TPD + 2 * HALO
    tile_index = jnp.arange(TILES, dtype=jnp.int32)
    owner = tile_index // TPD
    offsets = jnp.arange(cand_width, dtype=jnp.int32)
    candidate = owner[:, None] * TPD - HALO + offsets[None, :]
    usable = (candidate >= 0) & (candidate < TILES)
    scores = jax.random.randint(pick_key, (TILES, cand_width), 0, 2 ** 16) * 64 + offsets[None, :]
    scores = jnp.where(candidate == tile_index[:, None], 2 ** 30, jnp.where(usable, scores, -1))
    top_scores, picked = lax.top_k(scores, KT)
    chosen = jnp.take_along_axis(candidate, picked, axis=1)
    lowest = jax.random.randint(low_key, (N_DOM,), 1, KT + 1)[owner]
    extra = jax.random.randint(spread_key, (TILES,), 0, 2 ** 20) % (KT + 1 - lowest)
    counts = lowest + extra
    forced = jax.random.randint(force_key, (N_DOM,), 0, TPD)[owner]
    counts = jnp.where(tile_index % TPD == forced, KT, counts)
    slot_index = jnp.arange(KT, dtype=jnp.int32)
    lists = jnp.where(slot_index[None, :] < counts[:, None], chosen, tile_index[:, None])
    return (lists.astype(jnp.int32), counts.astype(jnp.int32))


def draw_tile_list(key, part):
    return tile_plan(key)[0]


def draw_tile_count(key, part):
    return tile_plan(key)[1]


def far_plan(seed_key):
    base_key = jax.random.fold_in(seed_key, 5)
    count_key, perm_key, row_key, source_key, place_key = jax.random.split(base_key, 5)
    lowest = max(1, CAP // 4)
    counts = jax.random.randint(count_key, (N_DOM, N_DOM), lowest, CAP + 1)
    order = jax.random.permutation(perm_key, N_DOM)
    targets = jnp.arange(N_DOM, dtype=jnp.int32)
    counts = counts.at[order, targets].set(CAP)
    sending = jax.random.randint(row_key, (N_DOM, N_DOM, CAP), 0, NODE_DEV)
    sending = sending.at[0, 0, 0].set(NODE_DEV - 1).at[0, 0, 1].set(0)
    node_index = jnp.arange(NODES, dtype=jnp.int32)
    dest_part = node_index // NODE_DEV
    sources = jax.random.randint(source_key, (NODES, DEG), 0, N_DOM)
    places = jax.random.randint(place_key, (NODES, DEG), 0, 2 ** 20) % counts[sources, dest_part[:, None]]
    slots = sources * CAP + places
    leading = (node_index % NODE_DEV == 0)[:, None]
    edge_index = jnp.arange(DEG, dtype=jnp.int32)[None, :]
    anchor = (order[dest_part] * CAP)[:, None]
    slots = jnp.where(leading & (edge_index == 0), anchor + CAP - 1, slots)
    slots = jnp.where(leading & (edge_index == 1), anchor, slots)
    return (sending.astype(jnp.int32), slots.astype(jnp.int32))


def draw_send_rows(key, part):
    return far_plan(key)[0]


def draw_expander_slot(key, part):
    return far_plan(key)[1]


def spiked(drawn, key, source, target, shards_of, factor):
    def block_of(position):
        return (jnp.arange(drawn.shape[position]) // (drawn.shape[position] // shards_of)).reshape((-1,) + (1,) * (drawn.ndim - 1 - position))

    first = jax.random.permutation(key, shards_of)[block_of(target)]
    other_side = (block_of(target) + shards_of // 2) % shards_of
    return jnp.where((block_of(source) == first) | (block_of(source) == other_side), factor * drawn, drawn)


def level_of(own_key, extent, cuts, smallest, high):
    factor_of = 1.0
    for axis_at, shards_of in cuts:
        draws = jax.random.uniform(jax.random.fold_in(jax.random.fold_in(own_key, 6), axis_at), (shards_of,), jnp.float32, smallest / len(cuts), high / len(cuts))
        factor_of = factor_of * jnp.repeat(jnp.exp(draws), extent[axis_at] // shards_of).reshape((-1,) + (1,) * (len(extent) - 1 - axis_at))
    return factor_of


def noise(stream_key, shape, scale, reach, cuts=(), held_as=jnp.bfloat16):
    result = scale * jax.random.normal(stream_key, shape, jnp.float32)
    if cuts:
        result = result * level_of(stream_key, shape, cuts, -0.22, 0.18)
    return jnp.clip(result, -reach, reach).astype(held_as)


def noise_with(key, extent, scale, reach, pieces, heavy, held_as=jnp.bfloat16):
    values = scale * jax.random.normal(key, extent, jnp.float32)
    if pieces:
        values = values * level_of(key, extent, pieces, -0.22, 0.18)
    return jnp.clip(spiked(values, jax.random.fold_in(key, 3), *heavy), -reach, reach).astype(held_as)


def setup_inputs(seed: int = 0) -> dict:
    splits = jax.random.split(jax.random.key(seed), 11)
    query_rows = draw_query_rows(jax.random.fold_in(splits[10], 71), 0)
    key_rows = draw_key_rows(jax.random.fold_in(splits[10], 71), 0)
    value_rows = noise(splits[2], (NODES, D), 1.0, 6.0, ((0, 16), (1, 2)))
    out_weight = noise(splits[3], (D, D), D ** -0.5, 0.25, ((0, 2),))
    out_grad = noise_with(splits[4], (NODES, D), 1.0, 6.0, ((0, 16), (1, 2)), (0, 1, 16, 2.0))
    far_bias = jnp.clip(4.0 + 3.0 * jax.random.uniform(splits[5], (HEADS,), jnp.float32) ** level_of(splits[5], (HEADS,), ((0, 2),), -0.2, 0.2), 4.0, 7.0)
    tile_list = draw_tile_list(jax.random.fold_in(splits[10], 71), 0)
    tile_count = draw_tile_count(jax.random.fold_in(splits[10], 71), 0)
    send_rows = draw_send_rows(jax.random.fold_in(splits[10], 71), 0)
    expander_slot = draw_expander_slot(jax.random.fold_in(splits[10], 71), 0)
    return dict(query_rows=query_rows, key_rows=key_rows, value_rows=value_rows, out_weight=out_weight, out_grad=out_grad, far_bias=far_bias, tile_list=tile_list, tile_count=tile_count, send_rows=send_rows, expander_slot=expander_slot)


def rounded(values):
    return lax.optimization_barrier(values.astype(jnp.bfloat16)).astype(jnp.float32)


def reference(query_rows, key_rows, value_rows, out_weight, out_grad, far_bias, tile_list, tile_count, send_rows, expander_slot):
    head_size = D // HEADS
    score_scale = head_size ** -0.5
    node_index = jnp.arange(NODES, dtype=jnp.int32)
    dest_part = node_index // NODE_DEV
    source_part = (expander_slot // CAP).astype(jnp.int32)
    far_index = source_part * NODE_DEV + send_rows[source_part, dest_part[:, None], expander_slot % CAP]
    attn_grad = jnp.dot(out_grad, out_weight.T, preferred_element_type=jnp.float32).astype(jnp.bfloat16)
    tile_lanes = jnp.arange(TILE, dtype=jnp.int32)
    slot_index = jnp.arange(KT, dtype=jnp.int32)

    def advance(accum, tile):
        key_acc, value_acc = accum
        first_row = (tile * TILE).astype(jnp.int32)
        queries = lax.dynamic_slice_in_dim(query_rows, first_row, TILE, 0).astype(jnp.float32).reshape(TILE, HEADS, head_size)
        upstream = lax.dynamic_slice_in_dim(attn_grad, first_row, TILE, 0).astype(jnp.float32).reshape(TILE, HEADS, head_size)
        near_rows = (tile_list[tile][:, None] * TILE + tile_lanes[None, :]).reshape(-1).astype(jnp.int32)
        live_keys = jnp.repeat(slot_index < tile_count[tile], TILE)
        near_keys = key_rows[near_rows].astype(jnp.float32).reshape(-1, HEADS, head_size)
        near_values = value_rows[near_rows].astype(jnp.float32).reshape(-1, HEADS, head_size)
        far_rows = lax.dynamic_slice_in_dim(far_index, first_row, TILE, 0).astype(jnp.int32)
        far_keys = key_rows[far_rows].astype(jnp.float32).reshape(TILE, DEG, HEADS, head_size)
        far_values = value_rows[far_rows].astype(jnp.float32).reshape(TILE, DEG, HEADS, head_size)
        near_score = jnp.einsum("qhd,khd->hqk", queries, near_keys) * score_scale
        far_score = jnp.einsum("qhd,qehd->hqe", queries, far_keys) * score_scale + far_bias[:, None, None]
        row_max = jnp.maximum(jnp.max(jnp.where(live_keys, near_score, -jnp.inf), axis=2), jnp.max(far_score, axis=2))
        near_exp = jnp.where(live_keys, jnp.exp(near_score - row_max[:, :, None]), 0.0)
        far_exp = jnp.exp(far_score - row_max[:, :, None])
        row_sum = jnp.sum(near_exp, axis=2) + jnp.sum(far_exp, axis=2)
        mixed = jnp.einsum("hqk,khd->qhd", rounded(near_exp), near_values) + jnp.einsum("hqe,qehd->qhd", rounded(far_exp), far_values)
        attention = rounded(mixed / row_sum.T[:, :, None])
        delta_term = jnp.sum(upstream * attention, axis=2).T
        near_dprob = jnp.einsum("qhd,khd->hqk", upstream, near_values)
        far_dprob = jnp.einsum("qhd,qehd->hqe", upstream, far_values)
        near_prob = near_exp / row_sum[:, :, None]
        far_prob = far_exp / row_sum[:, :, None]
        near_dscore = rounded(near_prob * (near_dprob - delta_term[:, :, None]))
        far_dscore = rounded(far_prob * (far_dprob - delta_term[:, :, None]))
        query_grad = (jnp.einsum("hqk,khd->qhd", near_dscore, near_keys) + jnp.einsum("hqe,qehd->qhd", far_dscore, far_keys)) * score_scale
        near_kgrad = jnp.einsum("hqk,qhd->khd", near_dscore, queries) * score_scale
        near_vgrad = jnp.einsum("hqk,qhd->khd", rounded(near_prob), upstream)
        far_kgrad = jnp.einsum("hqe,qhd->qehd", far_dscore, queries) * score_scale
        far_vgrad = jnp.einsum("hqe,qhd->qehd", rounded(far_prob), upstream)
        flat_far = far_rows.reshape(-1)
        key_acc = key_acc.at[near_rows].add(near_kgrad.reshape(-1, D)).at[flat_far].add(far_kgrad.reshape(-1, D))
        value_acc = value_acc.at[near_rows].add(near_vgrad.reshape(-1, D)).at[flat_far].add(far_vgrad.reshape(-1, D))
        return (key_acc, value_acc), (attention.astype(jnp.bfloat16).reshape(TILE, D), query_grad.astype(jnp.bfloat16).reshape(TILE, D))

    zero_rows = jnp.zeros((NODES, D), jnp.float32)
    (key_acc, value_acc), (attn_tiles, qgrad_tiles) = lax.scan(advance, (zero_rows, zero_rows), jnp.arange(TILES, dtype=jnp.int32))
    attention_all = attn_tiles.reshape(NODES, D)
    layer_out = jnp.dot(attention_all, out_weight, preferred_element_type=jnp.float32).astype(jnp.bfloat16)
    out_weight_grad = jnp.dot(out_grad.T, attention_all, preferred_element_type=jnp.float32)
    return (layer_out, qgrad_tiles.reshape(NODES, D), key_acc.astype(jnp.bfloat16), value_acc.astype(jnp.bfloat16), out_weight_grad)
```

```python
import functools

import jax
import jax.numpy as jnp
from jax import lax
from jax.experimental import pallas as pl
from jax.experimental.pallas import tpu as pltpu
from jax.sharding import PartitionSpec as P

TILE = 128
MESH = pl.DeviceIdType.MESH
F32 = jnp.float32
BF16 = jnp.bfloat16


def dot(a, b):
    return jnp.dot(a, b, preferred_element_type=F32)


def dot_nt(a, b):
    return lax.dot_general(a, b, (((1,), (1,)), ((), ())), preferred_element_type=F32)


def dot_tn(a, b):
    return lax.dot_general(a, b, (((0,), (0,)), ((), ())), preferred_element_type=F32)


def split_dot(x, m):
    hi = x.astype(BF16)
    lo = (x - hi.astype(F32)).astype(BF16)
    return dot(hi, m) + dot(lo, m)


def iota(shape, dim):
    return lax.broadcasted_iota(jnp.int32, shape, dim)


def slabs(flat, count, rows):
    return flat.reshape(count, rows, flat.shape[1])


def flat_of(stack):
    count, rows, width = stack.shape
    if rows % 16:
        return stack.astype(F32).reshape(count * rows, width).astype(BF16)
    return stack.reshape(count * rows, width)


def body(
    n, q_ref, k_ref, v_ref, w_ref, g_ref, bias_ref, list_ref, count_ref, rows_ref, slot_ref,
    lo_ref, qg_ref, kg_ref, vg_ref, dw_ref,
    kx, vx, out_far, in_far, back_out, back_in, g_oth, w_oth, att_mine, att_oth,
    rim_out, rim_in, dw_out, dw_in, exps, dprobs, mask_s, near_mix, near_max, near_sum,
    kgrad, vgrad, qgrad, far_t, rows_t, da_s, wide,
    far_ss, far_rs, rim_ss, rim_rs, bck_ss, bck_rs, rbk_ss, rbk_rs, dw_ss, dw_rs, hd_ss, hd_rs,
):
    me = lax.axis_index("dom")
    hd = lax.axis_index("head")
    nodes, cw = q_ref.shape
    heads = bias_ref.shape[0]
    hsize = cw // heads
    scale = hsize ** (-0.5)
    cap = out_far.shape[1]
    slots = n * cap
    deg = slot_ref.shape[1]
    tpd = nodes // TILE
    drows = dw_ref.shape[0]
    prev, nxt = lax.rem(me + n - 1, n), lax.rem(me + 1, n)

    barrier = pltpu.get_barrier_semaphore()

    def greet(i, _):
        pl.semaphore_signal(barrier, inc=1, device_id={"dom": lax.rem(me + i, n)}, device_id_type=MESH)
        return _

    lax.fori_loop(1, n, greet, 0)
    pl.semaphore_signal(barrier, inc=1, device_id={"head": 1 - hd}, device_id_type=MESH)
    pl.semaphore_wait(barrier, n)

    def to_dom(src, dst, ss, rs, d):
        return pltpu.make_async_remote_copy(
            src_ref=src, dst_ref=dst, send_sem=ss, recv_sem=rs, device_id={"dom": d}, device_id_type=MESH
        )

    def to_head(src, dst, i):
        return pltpu.make_async_remote_copy(
            src_ref=src, dst_ref=dst, send_sem=hd_ss.at[i], recv_sem=hd_rs.at[i],
            device_id={"head": 1 - hd}, device_id_type=MESH,
        )

    my_cols = pl.ds(pl.multiple_of(hd * cw, cw), cw)
    oth_cols = pl.ds(pl.multiple_of((1 - hd) * cw, cw), cw)
    send_g = to_head(g_ref, g_oth, 0)
    send_w = to_head(w_ref.at[:, oth_cols], w_oth, 1)
    send_att = to_head(att_mine, att_oth, 2)

    def rim_copies(low):
        d, at = (prev, 2) if low else (nxt, 0)
        s = 0 if low else 2
        return (
            to_dom(k_ref, kx.at[at], rim_ss.at[s], rim_rs.at[s], d),
            to_dom(v_ref, vx.at[at], rim_ss.at[s + 1], rim_rs.at[s + 1], d),
        )

    def rim_back(low):
        d, s = (prev, 0) if low else (nxt, 1)
        return to_dom(rim_out.at[s], rim_in.at[1 - s], rbk_ss.at[s], rbk_rs.at[s], d)

    def far_copy(d, s):
        return to_dom(out_far.at[d], in_far.at[s], far_ss.at[d], far_rs.at[s], d)

    def back_copy(d, s):
        return to_dom(back_out.at[d], back_in.at[s], bck_ss.at[d], bck_rs.at[s], d)

    def dw_copy(d, s):
        return to_dom(dw_out.at[d], dw_in.at[s], dw_ss.at[d], dw_rs.at[s], d)

    def every(fn):
        def step(i, _):
            fn(lax.rem(me + i, n))
            return _

        lax.fori_loop(1, n, step, 0)

    kv = jnp.concatenate([k_ref[...], v_ref[...]], axis=1)
    row_col = jnp.transpose(jnp.broadcast_to(rows_ref[...], (128, slots)))[:, 0:1]
    pick = (row_col == iota((slots, nodes), 1)).astype(F32).astype(BF16)
    picked = dot(pick, kv)
    if cap % 16:
        out_far[...] = slabs(picked, n, cap).astype(BF16)
    else:
        out_far[...] = slabs(picked.astype(BF16), n, cap)
    every(lambda d: far_copy(d, me).start())
    send_g.start()

    @pl.when(me > 0)
    def _():
        for c in rim_copies(True):
            c.start()

    @pl.when(me < n - 1)
    def _():
        for c in rim_copies(False):
            c.start()

    send_w.start()
    in_far[pl.ds(me, 1)] = out_far[pl.ds(me, 1)]

    kx[1] = k_ref[...]
    vx[1] = v_ref[...]

    @pl.when(me == 0)
    def _():
        kx[0] = jnp.zeros((nodes, cw), BF16)
        vx[0] = jnp.zeros((nodes, cw), BF16)
        rim_in[0] = jnp.zeros(rim_in.shape[1:], BF16)

    @pl.when(me == n - 1)
    def _():
        kx[2] = jnp.zeros((nodes, cw), BF16)
        vx[2] = jnp.zeros((nodes, cw), BF16)
        rim_in[1] = jnp.zeros(rim_in.shape[1:], BF16)

    rows_t[...] = (rows_ref[...] == iota((nodes, slots), 0)).astype(F32).astype(BF16)
    for e in range(deg):
        col = slot_ref[:, e : e + 1]
        row = jnp.transpose(jnp.broadcast_to(col, (nodes, 128)))[0:1, :]
        far_t[:, e * nodes : (e + 1) * nodes] = (row == iota((slots, nodes), 0)).astype(F32).astype(BF16)
    for t in range(tpd):
        for c in range(3 * tpd):
            live = jnp.int32(0)
            for j in range(list_ref.shape[1]):
                hit = (list_ref[t, j] == me * tpd + (c - tpd)) & (j < count_ref[t])
                live = jnp.maximum(live, hit.astype(jnp.int32))
            off = (1 - live).astype(F32) * jnp.float32(-1e30)
            mask_s[t * TILE : (t + 1) * TILE, c * TILE : (c + 1) * TILE] = jnp.full((TILE, TILE), off, F32)

    send_g.wait_recv()
    da_s[...] = (dot_nt(g_ref[...], w_ref[:, my_cols]) + dot_nt(g_oth[...], w_ref[:, oth_cols])).astype(BF16)
    lane = iota((nodes, 128), 1)
    col_head = iota((nodes, cw), 1) // hsize
    near_mix[...] = jnp.zeros((nodes, cw), F32)
    near_max[...] = jnp.zeros((nodes, 128), F32)
    near_sum[...] = jnp.ones((nodes, 128), F32)

    @pl.when(me > 0)
    def _():
        for c in rim_copies(False):
            c.wait_recv()

    @pl.when(me < n - 1)
    def _():
        for c in rim_copies(True):
            c.wait_recv()

    ext = 3 * nodes

    def near_head(h, _):
        here = col_head == h
        keys = kx[...].reshape(ext, cw)
        values = vx[...].reshape(ext, cw)
        qh = jnp.where(here, q_ref[...], jnp.zeros((), BF16))
        dah = jnp.where(here, da_s[...], jnp.zeros((), BF16))
        score = dot_nt(qh, keys) * scale + mask_s[...]
        top = jnp.max(score, axis=1, keepdims=True)
        ex = jnp.exp(score - top)
        exps[h] = ex
        near_max[...] = jnp.where(lane == h, top, near_max[...])
        near_sum[...] = jnp.where(lane == h, jnp.sum(ex, axis=1, keepdims=True), near_sum[...])
        near_mix[...] = jnp.where(here, dot(ex.astype(BF16), values), near_mix[...])
        dprobs[h] = dot_nt(dah, values)
        return _

    lax.fori_loop(0, heads, near_head, 0)

    every(lambda s: far_copy(s, s).wait_recv())
    fold = (iota((cw, 128), 0) // hsize == iota((cw, 128), 1)).astype(F32).astype(BF16)
    spread = (iota((128, cw), 0) == iota((128, cw), 1) // hsize).astype(F32).astype(BF16)
    bias = jnp.zeros((1, 128), F32)
    for h in range(heads):
        bias = jnp.where(iota((1, 128), 1) == h, bias_ref[h], bias)
    received = flat_of(in_far[...])
    q32 = q_ref[...].astype(F32)
    da32 = da_s[...].astype(F32)
    far_s = []
    for e in range(deg):
        hot = (slot_ref[:, e : e + 1] == iota((nodes, slots), 1)).astype(F32).astype(BF16)
        wide[e] = dot(hot, received)
        far_s.append(split_dot(q32 * wide[e, :, :cw], fold) * scale + bias)
    top_n = near_max[...]
    top = top_n
    for s in far_s:
        top = jnp.maximum(top, s)
    near_f = jnp.exp(top_n - top)
    far_x = [jnp.exp(s - top) for s in far_s]
    total = near_sum[...] * near_f
    for x in far_x:
        total = total + x
    inv = 1.0 / total
    mixed = near_mix[...] * split_dot(near_f, spread)
    for e in range(deg):
        mixed = mixed + dot(far_x[e].astype(BF16), spread) * wide[e, :, cw:]
    att = (mixed * split_dot(inv, spread)).astype(BF16)
    att_mine[...] = att
    send_att.start()
    delta = split_dot(da32 * att.astype(F32), fold)
    qg = jnp.zeros((nodes, cw), F32)
    parts = []
    for e in range(deg):
        prob = far_x[e] * inv
        dp = split_dot(da32 * wide[e, :, cw:], fold)
        ds = dot((prob * (dp - delta)).astype(BF16), spread)
        qg = qg + ds * wide[e, :, :cw]
        parts.append(
            jnp.concatenate(
                [(ds * q32 * scale).astype(BF16), (dot(prob.astype(BF16), spread) * da32).astype(BF16)], axis=1
            )
        )
    qgrad[...] = qg
    slot_grad = dot(far_t[...], jnp.concatenate(parts, axis=0))
    if cap % 16:
        back_out[...] = slabs(slot_grad, n, cap).astype(BF16)
    else:
        back_out[...] = slabs(slot_grad.astype(BF16), n, cap)
    every(lambda d: back_copy(d, me).start())
    back_in[pl.ds(me, 1)] = back_out[pl.ds(me, 1)]

    kgrad[...] = jnp.zeros((ext, cw), F32)
    vgrad[...] = jnp.zeros((ext, cw), F32)
    near_c = near_f * inv

    def near_back(h, _):
        here = col_head == h
        keys = kx[...].reshape(ext, cw)
        qh = jnp.where(here, q_ref[...], jnp.zeros((), BF16))
        dah = jnp.where(here, da_s[...], jnp.zeros((), BF16))
        c = jnp.sum(jnp.where(lane == h, near_c, 0.0), axis=1, keepdims=True)
        dl = jnp.sum(jnp.where(lane == h, delta, 0.0), axis=1, keepdims=True)
        prob = exps[h] * c
        ds = (prob * (dprobs[h] - dl)).astype(BF16)
        qgrad[...] += jnp.where(here, dot(ds, keys), 0.0)
        kgrad[...] += dot_tn(ds, qh)
        vgrad[...] += dot_tn(prob.astype(BF16), dah)
        return _

    lax.fori_loop(0, heads, near_back, 0)
    for s, lo in ((0, 0), (1, 2 * nodes)):
        rim_out[s, :, :cw] = (kgrad[lo : lo + nodes, :] * scale).astype(BF16)
        rim_out[s, :, cw:] = vgrad[lo : lo + nodes, :].astype(BF16)

    @pl.when(me > 0)
    def _():
        rim_back(True).start()

    @pl.when(me < n - 1)
    def _():
        rim_back(False).start()

    half = n // 2
    for mine in (True, False):
        block = dot_tn(g_ref[...] if mine else g_oth[...], att)
        first = (hd if mine else 1 - hd) * half
        if drows % 16:
            wide[0, :, :cw] = block
            for i in range(half):
                dw_out[pl.ds(first + i, 1)] = wide[0, i * drows : (i + 1) * drows, :cw].astype(BF16)[None]
        else:
            dw_out[pl.ds(first, half)] = slabs(block.astype(BF16), half, drows)
    every(lambda d: dw_copy(d, me).start())
    dw_in[pl.ds(me, 1)] = dw_out[pl.ds(me, 1)]

    qg_ref[...] = (qgrad[...] * scale).astype(BF16)
    send_w.wait_recv()
    send_att.wait_recv()
    lo_ref[...] = (dot(att, w_ref[:, my_cols]) + dot(att_oth[...], w_oth[...])).astype(BF16)

    @pl.when(me > 0)
    def _():
        rim_back(False).wait_recv()

    @pl.when(me < n - 1)
    def _():
        rim_back(True).wait_recv()

    every(lambda s: back_copy(s, s).wait_recv())
    own = dot(rows_t[...], flat_of(back_in[...]))
    rim = rim_in[0].astype(F32) + rim_in[1].astype(F32)
    own_k = kgrad[nodes : 2 * nodes, :] * scale
    kg_ref[...] = (own[:, :cw] + rim[:, :cw] + own_k).astype(BF16)
    vg_ref[...] = (own[:, cw:] + rim[:, cw:] + vgrad[nodes : 2 * nodes, :]).astype(BF16)
    every(lambda s: dw_copy(s, s).wait_recv())
    dw_ref[...] = jnp.sum(dw_in[...].astype(F32), axis=0)

    def left(d):
        far_copy(d, me).wait_send()
        back_copy(d, me).wait_send()
        dw_copy(d, me).wait_send()

    every(left)
    send_g.wait_send()
    send_w.wait_send()
    send_att.wait_send()

    @pl.when(me > 0)
    def _():
        for c in rim_copies(True):
            c.wait_send()
        rim_back(True).wait_send()

    @pl.when(me < n - 1)
    def _():
        for c in rim_copies(False):
            c.wait_send()
        rim_back(False).wait_send()


def shards(
    n, q, k, v, out_weight, out_grad, far_bias, tile_list, tile_count, send_rows, expander_slot
):
    nodes, cw = q.shape
    heads = far_bias.shape[0]
    cap = send_rows.shape[2]
    deg = expander_slot.shape[1]
    drows = 2 * cw // n
    ext = 3 * nodes
    slots = n * cap
    dma = pltpu.SemaphoreType.DMA
    vm = pl.BlockSpec(memory_space=pltpu.VMEM)
    sm = pl.BlockSpec(memory_space=pltpu.SMEM)
    node_out = jax.ShapeDtypeStruct((nodes, cw), BF16)
    return pl.pallas_call(
        functools.partial(body, n),
        out_shape=(node_out, node_out, node_out, node_out, jax.ShapeDtypeStruct((drows, cw), F32)),
        in_specs=[vm, vm, vm, vm, vm, sm, sm, sm, vm, vm],
        out_specs=(vm, vm, vm, vm, vm),
        scratch_shapes=[
            pltpu.VMEM((3, nodes, cw), BF16),
            pltpu.VMEM((3, nodes, cw), BF16),
            pltpu.VMEM((n, cap, 2 * cw), BF16),
            pltpu.VMEM((n, cap, 2 * cw), BF16),
            pltpu.VMEM((n, cap, 2 * cw), BF16),
            pltpu.VMEM((n, cap, 2 * cw), BF16),
            pltpu.VMEM((nodes, cw), BF16),
            pltpu.VMEM((cw, cw), BF16),
            pltpu.VMEM((nodes, cw), BF16),
            pltpu.VMEM((nodes, cw), BF16),
            pltpu.VMEM((2, nodes, 2 * cw), BF16),
            pltpu.VMEM((2, nodes, 2 * cw), BF16),
            pltpu.VMEM((n, drows, cw), BF16),
            pltpu.VMEM((n, drows, cw), BF16),
            pltpu.VMEM((heads, nodes, ext), F32),
            pltpu.VMEM((heads, nodes, ext), F32),
            pltpu.VMEM((nodes, ext), F32),
            pltpu.VMEM((nodes, cw), F32),
            pltpu.VMEM((nodes, 128), F32),
            pltpu.VMEM((nodes, 128), F32),
            pltpu.VMEM((ext, cw), F32),
            pltpu.VMEM((ext, cw), F32),
            pltpu.VMEM((nodes, cw), F32),
            pltpu.VMEM((slots, deg * nodes), BF16),
            pltpu.VMEM((nodes, slots), BF16),
            pltpu.VMEM((nodes, cw), BF16),
            pltpu.VMEM((deg, nodes, 2 * cw), F32),
            dma((n,)), dma((n,)), dma((4,)), dma((4,)), dma((n,)), dma((n,)),
            dma((2,)), dma((2,)), dma((n,)), dma((n,)), dma((3,)), dma((3,)),
        ],
        compiler_params=pltpu.CompilerParams(
            collective_id=0, has_side_effects=True, vmem_limit_bytes=48 * 1024 * 1024
        ),
        name="exphormer",
    )(
        q, k, v, out_weight, out_grad, far_bias, tile_list, tile_count,
        send_rows.reshape(1, slots), expander_slot,
    )


def solution(mesh):
    in_specs = (
        P("dom", "head"),
        P("dom", "head"),
        P("dom", "head"),
        P("head", None),
        P("dom", "head"),
        P("head"),
        P("dom", None),
        P("dom"),
        P("dom", None, None),
        P("dom", None),
    )
    out_specs = (P("dom", "head"),) * 5
    return jax.shard_map(
        functools.partial(shards, mesh.shape["dom"]),
        mesh=mesh, in_specs=in_specs, out_specs=out_specs, check_vma=False,
    )
```

```python
import functools
import math

import jax
import jax.numpy as jnp
from jax import lax
from jax.experimental import pallas as pl
from jax.experimental.pallas import tpu as pltpu
from jax.sharding import PartitionSpec as P

TILE = 128
MESH = pl.DeviceIdType.MESH
F32 = jnp.float32
BF16 = jnp.bfloat16


def dot(a, b):
    return jnp.dot(a, b, preferred_element_type=F32)


def dot_nt(a, b):
    return lax.dot_general(a, b, (((1,), (1,)), ((), ())), preferred_element_type=F32)


def dot_tn(a, b):
    return lax.dot_general(a, b, (((0,), (0,)), ((), ())), preferred_element_type=F32)


def split_dot(x, m):
    hi = x.astype(BF16)
    lo = (x - hi.astype(F32)).astype(BF16)
    return dot(hi, m) + dot(lo, m)


def iota(shape, dim):
    return lax.broadcasted_iota(jnp.int32, shape, dim)


def slabs(flat, count, rows):
    return flat.reshape(count, rows, flat.shape[1])


def flat_of(stack):
    count, rows, width = stack.shape
    if rows % 16:
        return stack.astype(F32).reshape(count * rows, width).astype(BF16)
    return stack.reshape(count * rows, width)


def body(
    n, q_hbm, k_hbm, v_hbm, w_hbm, g_hbm, bias_ref, list_ref, count_ref, send_ref, slot_ref,
    lo_ref, qg_ref, kg_ref, vg_ref, dw_ref,
    q_ref, w_ref, g_ref, rows_ref, hots, kx, vx, out_far, in_far, back_out, back_in, g_oth, w_oth, att_mine, att_oth,
    rim_out, rim_in, dw_out, dw_in, dw2_out, dw2_in, exps, dprobs, far_grad, mask_s, near_mix, near_max, near_sum,
    kgrad, vgrad, qgrad, far_t, rows_t, da_s, wide,
    far_ss, far_rs, rim_ss, rim_rs, bck_ss, bck_rs, rbk_ss, rbk_rs, dw_ss, dw_rs, dw2_ss, dw2_rs, hd_ss, hd_rs,
    in_sem,
):
    me = lax.axis_index("dom")
    hd = lax.axis_index("head")
    nodes, cw = q_hbm.shape
    heads = bias_ref.shape[0]
    hsize = cw // heads
    scale = hsize ** (-0.5)
    cap = out_far.shape[1]
    slots = n * cap
    deg = slot_ref.shape[1]
    tpd = nodes // TILE
    drows = dw_ref.shape[0]
    inner = dw_out.shape[0]
    outer = n // inner
    prev, nxt = lax.rem(me + n - 1, n), lax.rem(me + 1, n)

    loads = [
        pltpu.make_async_copy(src, dst, in_sem.at[i])
        for i, (src, dst) in enumerate(
            (
                (k_hbm, kx.at[1]),
                (v_hbm, vx.at[1]),
                (g_hbm, g_ref),
                (w_hbm, w_ref),
                (q_hbm, q_ref),
            )
        )
    ]
    for c in loads:
        c.start()

    barrier = pltpu.get_barrier_semaphore()

    def greet(i, _):
        pl.semaphore_signal(barrier, inc=1, device_id={"dom": lax.rem(me + i, n)}, device_id_type=MESH)
        return _

    lax.fori_loop(1, n, greet, 0)
    pl.semaphore_signal(barrier, inc=1, device_id={"head": 1 - hd}, device_id_type=MESH)
    pl.semaphore_wait(barrier, n)

    def to_dom(src, dst, ss, rs, d):
        return pltpu.make_async_remote_copy(
            src_ref=src, dst_ref=dst, send_sem=ss, recv_sem=rs, device_id={"dom": d}, device_id_type=MESH
        )

    def to_head(src, dst, i):
        return pltpu.make_async_remote_copy(
            src_ref=src, dst_ref=dst, send_sem=hd_ss.at[i], recv_sem=hd_rs.at[i],
            device_id={"head": 1 - hd}, device_id_type=MESH,
        )

    my_cols = pl.ds(pl.multiple_of(hd * cw, cw), cw)
    oth_cols = pl.ds(pl.multiple_of((1 - hd) * cw, cw), cw)
    send_g = to_head(g_ref, g_oth, 0)
    send_w = to_head(w_ref.at[:, oth_cols], w_oth, 1)
    send_att = to_head(att_mine, att_oth, 2)

    def rim_copies(low):
        d, at = (prev, 2) if low else (nxt, 0)
        s = 0 if low else 2
        return (
            to_dom(kx.at[1], kx.at[at], rim_ss.at[s], rim_rs.at[s], d),
            to_dom(vx.at[1], vx.at[at], rim_ss.at[s + 1], rim_rs.at[s + 1], d),
        )

    def rim_back(low):
        d, s = (prev, 0) if low else (nxt, 1)
        return to_dom(rim_out.at[s], rim_in.at[1 - s], rbk_ss.at[s], rbk_rs.at[s], d)

    def far_copy(d, s):
        return to_dom(out_far.at[d], in_far.at[s], far_ss.at[d], far_rs.at[s], d)

    def back_copy(d, s):
        return to_dom(back_out.at[d], back_in.at[s], bck_ss.at[d], bck_rs.at[s], d)

    my_in, my_out = lax.rem(me, inner), me // inner

    def dw_copy(j, s):
        return to_dom(dw_out.at[j], dw_in.at[s], dw_ss.at[j], dw_rs.at[s], my_out * inner + j)

    def dw2_copy(o, s):
        return to_dom(dw2_out.at[o], dw2_in.at[s], dw2_ss.at[o], dw2_rs.at[s], o * inner + my_in)

    def partner(a, i, size):
        if size & (size - 1):
            return lax.rem(a + i, size)
        bit, out = 1, 0
        while bit < size:
            out = out + ((a // bit + i // bit) % 2) * bit
            bit *= 2
        return out

    def every(fn, at=None, size=n):
        at = me if at is None else at

        def step(i, _):
            fn(partner(at, i, size))
            return _

        lax.fori_loop(1, size, step, 0)

    rows_ref[...] = jnp.zeros(rows_ref.shape, jnp.int32)
    rows_ref[:n, :cap] = send_ref[0]
    for c in loads[:2]:
        c.wait()

    @pl.when(me > 0)
    def _():
        for c in rim_copies(True):
            c.start()

    @pl.when(me < n - 1)
    def _():
        for c in rim_copies(False):
            c.start()

    loads[2].wait()
    send_g.start()
    kv = jnp.concatenate([kx[1], vx[1]], axis=1)
    row_cols = jnp.transpose(rows_ref[...])
    row_col = jnp.concatenate([row_cols[:cap, d : d + 1] for d in range(n)], axis=0)
    pick = (row_col == iota((slots, nodes), 1)).astype(F32)
    picked = dot(pick.astype(BF16), kv)
    if cap % 16:
        out_far[...] = slabs(picked, n, cap).astype(BF16)
    else:
        out_far[...] = slabs(picked.astype(BF16), n, cap)
    every(lambda d: far_copy(d, me).start())

    loads[3].wait()
    send_w.start()
    loads[4].wait()
    in_far[pl.ds(me, 1)] = out_far[pl.ds(me, 1)]

    @pl.when(me == 0)
    def _():
        kx[0] = jnp.zeros((nodes, cw), BF16)
        vx[0] = jnp.zeros((nodes, cw), BF16)
        rim_in[0] = jnp.zeros(rim_in.shape[1:], BF16)

    @pl.when(me == n - 1)
    def _():
        kx[2] = jnp.zeros((nodes, cw), BF16)
        vx[2] = jnp.zeros((nodes, cw), BF16)
        rim_in[1] = jnp.zeros(rim_in.shape[1:], BF16)

    rows_t[...] = jnp.transpose(pick).astype(BF16)
    for e in range(deg):
        col = slot_ref[:, e : e + 1]
        hots[e] = (col == iota((nodes, slots), 1)).astype(F32).astype(BF16)
        row = jnp.transpose(jnp.broadcast_to(col, (nodes, 128)))[0:1, :]
        far_t[:, e * nodes : (e + 1) * nodes] = (row == iota((slots, nodes), 0)).astype(F32).astype(BF16)
    for t in range(tpd):
        for c in range(3 * tpd):
            live = jnp.int32(0)
            for j in range(list_ref.shape[1]):
                hit = (list_ref[t, j] == me * tpd + (c - tpd)) & (j < count_ref[t])
                live = jnp.maximum(live, hit.astype(jnp.int32))
            off = (1 - live).astype(F32) * jnp.float32(-1e30)
            mask_s[t * TILE : (t + 1) * TILE, c * TILE : (c + 1) * TILE] = jnp.full((TILE, TILE), off, F32)

    send_g.wait_recv()
    da_s[...] = (dot_nt(g_ref[...], w_ref[:, my_cols]) + dot_nt(g_oth[...], w_ref[:, oth_cols])).astype(BF16)
    lane = iota((nodes, 128), 1)
    col_head = iota((nodes, cw), 1) // hsize
    near_mix[...] = jnp.zeros((nodes, cw), F32)
    near_max[...] = jnp.zeros((nodes, 128), F32)
    near_sum[...] = jnp.ones((nodes, 128), F32)

    @pl.when(me > 0)
    def _():
        for c in rim_copies(False):
            c.wait_recv()

    @pl.when(me < n - 1)
    def _():
        for c in rim_copies(True):
            c.wait_recv()

    ext = 3 * nodes

    def near_head(h, _):
        here = col_head == h
        keys = kx[...].reshape(ext, cw)
        values = vx[...].reshape(ext, cw)
        qh = jnp.where(here, q_ref[...], jnp.zeros((), BF16))
        dah = jnp.where(here, da_s[...], jnp.zeros((), BF16))
        score = dot_nt(qh, keys) * scale + mask_s[...]
        top = jnp.max(score, axis=1, keepdims=True)
        ex = jnp.exp(score - top)
        exps[h] = ex
        near_max[...] = jnp.where(lane == h, top, near_max[...])
        near_sum[...] = jnp.where(lane == h, jnp.sum(ex, axis=1, keepdims=True), near_sum[...])
        near_mix[...] = jnp.where(here, dot(ex.astype(BF16), values), near_mix[...])
        dprobs[h] = dot_nt(dah, values)
        return _

    lax.fori_loop(0, heads, near_head, 0)

    fold = (iota((cw, 128), 0) // hsize == iota((cw, 128), 1)).astype(F32).astype(BF16)
    spread = (iota((128, cw), 0) == iota((128, cw), 1) // hsize).astype(F32).astype(BF16)
    bias = jnp.zeros((1, 128), F32)
    for h in range(heads):
        bias = jnp.where(iota((1, 128), 1) == h, bias_ref[h], bias)
    q32 = q_ref[...].astype(F32)
    da32 = da_s[...].astype(F32)
    every(lambda s: far_copy(s, s).wait_recv())
    received = flat_of(in_far[...])
    far_s = []
    for e in range(deg):
        wide[e] = dot(hots[e], received)
        far_s.append(split_dot(q32 * wide[e, :, :cw], fold) * scale + bias)
    top_n = near_max[...]
    top = top_n
    for s in far_s:
        top = jnp.maximum(top, s)
    near_f = jnp.exp(top_n - top)
    far_x = [jnp.exp(s - top) for s in far_s]
    total = near_sum[...] * near_f
    for x in far_x:
        total = total + x
    inv = 1.0 / total
    mixed = near_mix[...] * split_dot(near_f, spread)
    for e in range(deg):
        mixed = mixed + dot(far_x[e].astype(BF16), spread) * wide[e, :, cw:]
    att = (mixed * split_dot(inv, spread)).astype(BF16)
    att_mine[...] = att
    send_att.start()
    delta = split_dot(da32 * att.astype(F32), fold)
    qg = jnp.zeros((nodes, cw), F32)
    parts = []
    for e in range(deg):
        prob = far_x[e] * inv
        dp = split_dot(da32 * wide[e, :, cw:], fold)
        ds = dot((prob * (dp - delta)).astype(BF16), spread)
        qg = qg + ds * wide[e, :, :cw]
        parts.append(
            jnp.concatenate(
                [(ds * q32 * scale).astype(BF16), (dot(prob.astype(BF16), spread) * da32).astype(BF16)], axis=1
            )
        )
    qgrad[...] = qg
    far_grad[...] = jnp.concatenate(parts, axis=0)
    group = inner * cap

    def send_back(i, _):
        o = partner(my_out, outer - 1 - i, outer)
        slot_grad = dot(far_t[pl.ds(pl.multiple_of(o * group, group), group), :], far_grad[...])
        if cap % 16:
            block = slabs(slot_grad, inner, cap).astype(BF16)
        else:
            block = slabs(slot_grad.astype(BF16), inner, cap)
        back_out[pl.ds(o * inner, inner)] = block
        for j in range(inner):
            d = o * inner + partner(my_in, j, inner)

            @pl.when(d != me)
            def go():
                back_copy(d, me).start()

        return _

    lax.fori_loop(0, outer, send_back, 0)
    back_in[pl.ds(me, 1)] = back_out[pl.ds(me, 1)]

    kgrad[...] = jnp.zeros((ext, cw), F32)
    vgrad[...] = jnp.zeros((ext, cw), F32)
    near_c = near_f * inv

    def near_back(h, _):
        here = col_head == h
        keys = kx[...].reshape(ext, cw)
        qh = jnp.where(here, q_ref[...], jnp.zeros((), BF16))
        dah = jnp.where(here, da_s[...], jnp.zeros((), BF16))
        c = jnp.sum(jnp.where(lane == h, near_c, 0.0), axis=1, keepdims=True)
        dl = jnp.sum(jnp.where(lane == h, delta, 0.0), axis=1, keepdims=True)
        prob = exps[h] * c
        ds = (prob * (dprobs[h] - dl)).astype(BF16)
        qgrad[...] += jnp.where(here, dot(ds, keys), 0.0)
        kgrad[...] += dot_tn(ds, qh)
        vgrad[...] += dot_tn(prob.astype(BF16), dah)
        return _

    lax.fori_loop(0, heads, near_back, 0)
    for s, lo in ((0, 0), (1, 2 * nodes)):
        rim_out[s, :, :cw] = (kgrad[lo : lo + nodes, :] * scale).astype(BF16)
        rim_out[s, :, cw:] = vgrad[lo : lo + nodes, :].astype(BF16)

    @pl.when(me > 0)
    def _():
        rim_back(True).start()

    @pl.when(me < n - 1)
    def _():
        rim_back(False).start()

    half = outer // 2
    for mine in (True, False):
        block = dot_tn(g_ref[...] if mine else g_oth[...], att)
        first = (hd if mine else 1 - hd) * half
        if drows % 16:
            wide[0, :, :cw] = block
            for i in range(half * inner):
                dw_out[i % inner, pl.ds(first + i // inner, 1)] = (
                    wide[0, i * drows : (i + 1) * drows, :cw].astype(BF16)[None]
                )
        else:
            cut = block.astype(BF16).reshape(half, inner, drows, cw)
            for j in range(inner):
                dw_out[j, pl.ds(first, half)] = cut[:, j]
    every(lambda j: dw_copy(j, my_in).start(), my_in, inner)
    dw_in[pl.ds(my_in, 1)] = dw_out[pl.ds(my_in, 1)]

    qg_ref[...] = (qgrad[...] * scale).astype(BF16)
    send_w.wait_recv()
    send_att.wait_recv()
    lo_ref[...] = (dot(att, w_ref[:, my_cols]) + dot(att_oth[...], w_oth[...])).astype(BF16)

    every(lambda s: dw_copy(s, s).wait_recv(), my_in, inner)
    dw2_out[...] = jnp.sum(dw_in[...].astype(F32), axis=0).astype(BF16)
    every(lambda o: dw2_copy(o, my_out).start(), my_out, outer)
    dw2_in[pl.ds(my_out, 1)] = dw2_out[pl.ds(my_out, 1)]

    @pl.when(me > 0)
    def _():
        rim_back(False).wait_recv()

    @pl.when(me < n - 1)
    def _():
        rim_back(True).wait_recv()

    every(lambda s: dw2_copy(s, s).wait_recv(), my_out, outer)
    dw_ref[...] = jnp.sum(dw2_in[...].astype(F32), axis=0)
    every(lambda s: back_copy(s, s).wait_recv())
    own = dot(rows_t[...], flat_of(back_in[...]))
    rim = rim_in[0].astype(F32) + rim_in[1].astype(F32)
    own_k = kgrad[nodes : 2 * nodes, :] * scale
    kg_ref[...] = (own[:, :cw] + rim[:, :cw] + own_k).astype(BF16)
    vg_ref[...] = (own[:, cw:] + rim[:, cw:] + vgrad[nodes : 2 * nodes, :]).astype(BF16)

    def left(d):
        far_copy(d, me).wait_send()
        back_copy(d, me).wait_send()

    every(left)
    every(lambda j: dw_copy(j, my_in).wait_send(), my_in, inner)
    every(lambda o: dw2_copy(o, my_out).wait_send(), my_out, outer)
    send_g.wait_send()
    send_w.wait_send()
    send_att.wait_send()

    @pl.when(me > 0)
    def _():
        for c in rim_copies(True):
            c.wait_send()
        rim_back(True).wait_send()

    @pl.when(me < n - 1)
    def _():
        for c in rim_copies(False):
            c.wait_send()
        rim_back(False).wait_send()


def place(*refs):
    for i in range(5):
        refs[5 + i][...] = refs[i][...]


def shards(
    n, q, k, v, out_weight, out_grad, far_bias, tile_list, tile_count, send_rows, expander_slot
):
    nodes, cw = q.shape
    heads = far_bias.shape[0]
    cap = send_rows.shape[2]
    deg = expander_slot.shape[1]
    drows = 2 * cw // n
    inner = math.gcd(n, 4)
    ext = 3 * nodes
    slots = n * cap
    dma = pltpu.SemaphoreType.DMA
    vm = pl.BlockSpec(memory_space=pltpu.VMEM)
    sm = pl.BlockSpec(memory_space=pltpu.SMEM)
    node_out = jax.ShapeDtypeStruct((nodes, cw), BF16)
    anywhere = pl.BlockSpec(memory_space=pl.ANY)
    outs = pl.pallas_call(
        functools.partial(body, n),
        out_shape=(node_out, node_out, node_out, node_out, jax.ShapeDtypeStruct((drows, cw), F32)),
        in_specs=[anywhere] * 5 + [sm] * 3 + [vm] * 2,
        out_specs=(vm, vm, vm, vm, vm),
        scratch_shapes=[
            pltpu.VMEM((nodes, cw), BF16),
            pltpu.VMEM((cw, 2 * cw), BF16),
            pltpu.VMEM((nodes, cw), BF16),
            pltpu.VMEM((128, 128), jnp.int32),
            pltpu.VMEM((deg, nodes, slots), BF16),
            pltpu.VMEM((3, nodes, cw), BF16),
            pltpu.VMEM((3, nodes, cw), BF16),
            pltpu.VMEM((n, cap, 2 * cw), BF16),
            pltpu.VMEM((n, cap, 2 * cw), BF16),
            pltpu.VMEM((n, cap, 2 * cw), BF16),
            pltpu.VMEM((n, cap, 2 * cw), BF16),
            pltpu.VMEM((nodes, cw), BF16),
            pltpu.VMEM((cw, cw), BF16),
            pltpu.VMEM((nodes, cw), BF16),
            pltpu.VMEM((nodes, cw), BF16),
            pltpu.VMEM((2, nodes, 2 * cw), BF16),
            pltpu.VMEM((2, nodes, 2 * cw), BF16),
            pltpu.VMEM((inner, n // inner, drows, cw), BF16),
            pltpu.VMEM((inner, n // inner, drows, cw), BF16),
            pltpu.VMEM((n // inner, drows, cw), BF16),
            pltpu.VMEM((n // inner, drows, cw), BF16),
            pltpu.VMEM((heads, nodes, ext), F32),
            pltpu.VMEM((heads, nodes, ext), F32),
            pltpu.VMEM((deg * nodes, 2 * cw), BF16),
            pltpu.VMEM((nodes, ext), F32),
            pltpu.VMEM((nodes, cw), F32),
            pltpu.VMEM((nodes, 128), F32),
            pltpu.VMEM((nodes, 128), F32),
            pltpu.VMEM((ext, cw), F32),
            pltpu.VMEM((ext, cw), F32),
            pltpu.VMEM((nodes, cw), F32),
            pltpu.VMEM((slots, deg * nodes), BF16),
            pltpu.VMEM((nodes, slots), BF16),
            pltpu.VMEM((nodes, cw), BF16),
            pltpu.VMEM((deg, nodes, 2 * cw), F32),
            dma((n,)), dma((n,)), dma((4,)), dma((4,)), dma((n,)), dma((n,)),
            dma((2,)), dma((2,)), dma((inner,)), dma((inner,)), dma((n // inner,)), dma((n // inner,)),
            dma((3,)), dma((3,)), dma((5,)),
        ],
        compiler_params=pltpu.CompilerParams(
            collective_id=0, has_side_effects=True, vmem_limit_bytes=60 * 1024 * 1024
        ),
        name="exphormer",
    )(
        q, k, v, out_weight, out_grad, far_bias, tile_list, tile_count,
        send_rows, expander_slot,
    )
    return pl.pallas_call(
        place,
        out_shape=tuple(jax.ShapeDtypeStruct(o.shape, o.dtype) for o in outs),
        in_specs=[vm] * 5,
        out_specs=(vm,) * 5,
        name="place",
    )(*outs)


def solution(mesh):
    in_specs = (
        P("dom", "head"),
        P("dom", "head"),
        P("dom", "head"),
        P("head", None),
        P("dom", "head"),
        P("head"),
        P("dom", None),
        P("dom"),
        P("dom", None, None),
        P("dom", None),
    )
    out_specs = (P("dom", "head"),) * 5
    return jax.shard_map(
        functools.partial(shards, mesh.shape["dom"]),
        mesh=mesh, in_specs=in_specs, out_specs=out_specs, check_vma=False,
    )
```

```python
import functools
import math

import jax
import jax.numpy as jnp
from jax import lax
from jax.experimental import pallas as pl
from jax.experimental.pallas import tpu as pltpu
from jax.sharding import PartitionSpec as P

TILE = 128
MESH = pl.DeviceIdType.MESH
F32 = jnp.float32
BF16 = jnp.bfloat16


def dot(a, b):
    return jnp.dot(a, b, preferred_element_type=F32)


def dot_nt(a, b):
    return lax.dot_general(a, b, (((1,), (1,)), ((), ())), preferred_element_type=F32)


def dot_tn(a, b):
    return lax.dot_general(a, b, (((0,), (0,)), ((), ())), preferred_element_type=F32)


def split_dot(x, m):
    hi = x.astype(BF16)
    lo = (x - hi.astype(F32)).astype(BF16)
    return dot(hi, m) + dot(lo, m)


def iota(shape, dim):
    return lax.broadcasted_iota(jnp.int32, shape, dim)


def slabs(flat, count, rows):
    return flat.reshape(count, rows, flat.shape[1])


def flat_of(stack):
    count, rows, width = stack.shape
    if rows % 16:
        return stack.astype(F32).reshape(count * rows, width).astype(BF16)
    return stack.reshape(count * rows, width)


def body(
    n, q_hbm, k_hbm, v_hbm, w_hbm, g_hbm, bias_ref, list_ref, count_ref, send_ref, slot_ref,
    lo_ref, qg_ref, kg_ref, vg_ref, dw_ref,
    q_ref, w_ref, g_ref, rows_ref, hots, kx, vx, out_far, in_far, back_out, back_in, g_oth, w_oth, att_mine, att_oth,
    rim_out, rim_in, dw_out, dw_in, dw2_out, dw2_in, exps, dprobs, far_grad, mask_s, near_mix, near_max, near_sum,
    kgrad, vgrad, qgrad, far_t, rows_t, da_s, wide,
    far_ss, far_rs, rim_ss, rim_rs, bck_ss, bck_rs, rbk_ss, rbk_rs, dw_ss, dw_rs, dw2_ss, dw2_rs, hd_ss, hd_rs,
    in_sem,
):
    me = lax.axis_index("dom")
    hd = lax.axis_index("head")
    nodes, cw = q_hbm.shape
    heads = bias_ref.shape[0]
    hsize = cw // heads
    scale = hsize ** (-0.5)
    cap = out_far.shape[1]
    slots = n * cap
    deg = slot_ref.shape[0]
    tpd = nodes // TILE
    drows = dw_ref.shape[0]
    inner = dw_out.shape[0]
    outer = n // inner
    prev, nxt = lax.rem(me + n - 1, n), lax.rem(me + 1, n)

    loads = [
        pltpu.make_async_copy(src, dst, in_sem.at[i])
        for i, (src, dst) in enumerate(
            (
                (k_hbm, kx.at[1]),
                (v_hbm, vx.at[1]),
                (g_hbm, g_ref),
                (w_hbm, w_ref),
                (q_hbm, q_ref),
            )
        )
    ]
    for c in loads:
        c.start()

    barrier = pltpu.get_barrier_semaphore()

    def greet(i, _):
        pl.semaphore_signal(barrier, inc=1, device_id={"dom": lax.rem(me + i, n)}, device_id_type=MESH)
        return _

    lax.fori_loop(1, n, greet, 0)
    pl.semaphore_signal(barrier, inc=1, device_id={"head": 1 - hd}, device_id_type=MESH)
    pl.semaphore_wait(barrier, n)

    def to_dom(src, dst, ss, rs, d):
        return pltpu.make_async_remote_copy(
            src_ref=src, dst_ref=dst, send_sem=ss, recv_sem=rs, device_id={"dom": d}, device_id_type=MESH
        )

    def to_head(src, dst, i):
        return pltpu.make_async_remote_copy(
            src_ref=src, dst_ref=dst, send_sem=hd_ss.at[i], recv_sem=hd_rs.at[i],
            device_id={"head": 1 - hd}, device_id_type=MESH,
        )

    my_cols = pl.ds(pl.multiple_of(hd * cw, cw), cw)
    oth_cols = pl.ds(pl.multiple_of((1 - hd) * cw, cw), cw)
    send_g = to_head(g_ref, g_oth, 0)
    send_w = to_head(w_ref.at[:, oth_cols], w_oth, 1)
    send_att = to_head(att_mine, att_oth, 2)

    def rim_copies(low):
        d, at = (prev, 2) if low else (nxt, 0)
        s = 0 if low else 2
        return (
            to_dom(kx.at[1], kx.at[at], rim_ss.at[s], rim_rs.at[s], d),
            to_dom(vx.at[1], vx.at[at], rim_ss.at[s + 1], rim_rs.at[s + 1], d),
        )

    def rim_back(low):
        d, s = (prev, 0) if low else (nxt, 1)
        return to_dom(rim_out.at[s], rim_in.at[1 - s], rbk_ss.at[s], rbk_rs.at[s], d)

    def far_copy(d, s):
        return to_dom(out_far.at[d], in_far.at[s], far_ss.at[d], far_rs.at[s], d)

    def back_copy(d, s):
        return to_dom(back_out.at[d], back_in.at[s], bck_ss.at[d], bck_rs.at[s], d)

    my_in, my_out = lax.rem(me, inner), me // inner

    def dw_copy(j, s):
        return to_dom(dw_out.at[j], dw_in.at[s], dw_ss.at[j], dw_rs.at[s], my_out * inner + j)

    def dw2_copy(o, s):
        return to_dom(dw2_out.at[o], dw2_in.at[s], dw2_ss.at[o], dw2_rs.at[s], o * inner + my_in)

    def partner(a, i, size):
        if size & (size - 1):
            return lax.rem(a + i, size)
        bit, out = 1, 0
        while bit < size:
            out = out + ((a // bit + i // bit) % 2) * bit
            bit *= 2
        return out

    def every(fn, at=None, size=n):
        at = me if at is None else at

        def step(i, _):
            fn(partner(at, i, size))
            return _

        lax.fori_loop(1, size, step, 0)

    rows_ref[...] = jnp.zeros(rows_ref.shape, jnp.int32)
    rows_ref[:n, :cap] = send_ref[0]
    for c in loads[:2]:
        c.wait()

    @pl.when(me > 0)
    def _():
        for c in rim_copies(True):
            c.start()

    @pl.when(me < n - 1)
    def _():
        for c in rim_copies(False):
            c.start()

    loads[2].wait()
    send_g.start()
    kv = jnp.concatenate([kx[1], vx[1]], axis=1)
    row_cols = jnp.transpose(rows_ref[...])
    row_col = jnp.concatenate([row_cols[:cap, d : d + 1] for d in range(n)], axis=0)
    pick = (row_col == iota((slots, nodes), 1)).astype(F32)
    picked = dot(pick.astype(BF16), kv)
    if cap % 16:
        out_far[...] = slabs(picked, n, cap).astype(BF16)
    else:
        out_far[...] = slabs(picked.astype(BF16), n, cap)
    every(lambda d: far_copy(d, me).start())

    loads[3].wait()
    send_w.start()
    loads[4].wait()
    in_far[pl.ds(me, 1)] = out_far[pl.ds(me, 1)]

    @pl.when(me == 0)
    def _():
        kx[0] = jnp.zeros((nodes, cw), BF16)
        vx[0] = jnp.zeros((nodes, cw), BF16)
        rim_in[0] = jnp.zeros(rim_in.shape[1:], BF16)

    @pl.when(me == n - 1)
    def _():
        kx[2] = jnp.zeros((nodes, cw), BF16)
        vx[2] = jnp.zeros((nodes, cw), BF16)
        rim_in[1] = jnp.zeros(rim_in.shape[1:], BF16)

    rows_t[...] = jnp.transpose(pick).astype(BF16)
    for e in range(deg):
        row = slot_ref[e : e + 1, :]
        col = jnp.transpose(jnp.broadcast_to(row, (128, nodes)))[:, 0:1]
        hots[e] = (col == iota((nodes, slots), 1)).astype(F32).astype(BF16)
        far_t[:, e * nodes : (e + 1) * nodes] = (row == iota((slots, nodes), 0)).astype(F32).astype(BF16)
    for t in range(tpd):
        for c in range(3 * tpd):
            live = jnp.int32(0)
            for j in range(list_ref.shape[1]):
                hit = (list_ref[t, j] == me * tpd + (c - tpd)) & (j < count_ref[t])
                live = jnp.maximum(live, hit.astype(jnp.int32))
            off = (1 - live).astype(F32) * jnp.float32(-1e30)
            mask_s[t * TILE : (t + 1) * TILE, c * TILE : (c + 1) * TILE] = jnp.full((TILE, TILE), off, F32)

    send_g.wait_recv()
    da_s[...] = (dot_nt(g_ref[...], w_ref[:, my_cols]) + dot_nt(g_oth[...], w_ref[:, oth_cols])).astype(BF16)
    lane = iota((nodes, 128), 1)
    col_head = iota((nodes, cw), 1) // hsize
    near_mix[...] = jnp.zeros((nodes, cw), F32)
    near_max[...] = jnp.zeros((nodes, 128), F32)
    near_sum[...] = jnp.ones((nodes, 128), F32)

    @pl.when(me > 0)
    def _():
        for c in rim_copies(False):
            c.wait_recv()

    @pl.when(me < n - 1)
    def _():
        for c in rim_copies(True):
            c.wait_recv()

    ext = 3 * nodes

    def near_head(h, _):
        here = col_head == h
        keys = kx[...].reshape(ext, cw)
        values = vx[...].reshape(ext, cw)
        qh = jnp.where(here, q_ref[...], jnp.zeros((), BF16))
        dah = jnp.where(here, da_s[...], jnp.zeros((), BF16))
        score = dot_nt(qh, keys) * scale + mask_s[...]
        top = jnp.max(score, axis=1, keepdims=True)
        ex = jnp.exp(score - top)
        exps[h] = ex
        near_max[...] = jnp.where(lane == h, top, near_max[...])
        near_sum[...] = jnp.where(lane == h, jnp.sum(ex, axis=1, keepdims=True), near_sum[...])
        near_mix[...] = jnp.where(here, dot(ex.astype(BF16), values), near_mix[...])
        dprobs[h] = dot_nt(dah, values)
        return _

    lax.fori_loop(0, heads, near_head, 0)

    fold = (iota((cw, 128), 0) // hsize == iota((cw, 128), 1)).astype(F32).astype(BF16)
    spread = (iota((128, cw), 0) == iota((128, cw), 1) // hsize).astype(F32).astype(BF16)
    bias = jnp.zeros((1, 128), F32)
    for h in range(heads):
        bias = jnp.where(iota((1, 128), 1) == h, bias_ref[h], bias)
    q32 = q_ref[...].astype(F32)
    da32 = da_s[...].astype(F32)
    every(lambda s: far_copy(s, s).wait_recv())
    received = flat_of(in_far[...])
    far_s = []
    for e in range(deg):
        wide[e] = dot(hots[e], received)
        far_s.append(split_dot(q32 * wide[e, :, :cw], fold) * scale + bias)
    top_n = near_max[...]
    top = top_n
    for s in far_s:
        top = jnp.maximum(top, s)
    near_f = jnp.exp(top_n - top)
    far_x = [jnp.exp(s - top) for s in far_s]
    total = near_sum[...] * near_f
    for x in far_x:
        total = total + x
    inv = 1.0 / total
    mixed = near_mix[...] * split_dot(near_f, spread)
    for e in range(deg):
        mixed = mixed + dot(far_x[e].astype(BF16), spread) * wide[e, :, cw:]
    att = (mixed * split_dot(inv, spread)).astype(BF16)
    att_mine[...] = att
    send_att.start()
    delta = split_dot(da32 * att.astype(F32), fold)
    qg = jnp.zeros((nodes, cw), F32)
    parts = []
    for e in range(deg):
        prob = far_x[e] * inv
        dp = split_dot(da32 * wide[e, :, cw:], fold)
        ds = dot((prob * (dp - delta)).astype(BF16), spread)
        qg = qg + ds * wide[e, :, :cw]
        parts.append(
            jnp.concatenate(
                [(ds * q32 * scale).astype(BF16), (dot(prob.astype(BF16), spread) * da32).astype(BF16)], axis=1
            )
        )
    qgrad[...] = qg
    far_grad[...] = jnp.concatenate(parts, axis=0)
    group = inner * cap

    def send_back(i, _):
        o = partner(my_out, outer - 1 - i, outer)
        slot_grad = dot(far_t[pl.ds(pl.multiple_of(o * group, group), group), :], far_grad[...])
        if cap % 16:
            block = slabs(slot_grad, inner, cap).astype(BF16)
        else:
            block = slabs(slot_grad.astype(BF16), inner, cap)
        back_out[pl.ds(o * inner, inner)] = block
        for j in range(inner):
            d = o * inner + partner(my_in, j, inner)

            @pl.when(d != me)
            def go():
                back_copy(d, me).start()

        return _

    lax.fori_loop(0, outer, send_back, 0)
    back_in[pl.ds(me, 1)] = back_out[pl.ds(me, 1)]

    kgrad[...] = jnp.zeros((ext, cw), F32)
    vgrad[...] = jnp.zeros((ext, cw), F32)
    near_c = near_f * inv

    def near_back(h, _):
        here = col_head == h
        keys = kx[...].reshape(ext, cw)
        qh = jnp.where(here, q_ref[...], jnp.zeros((), BF16))
        dah = jnp.where(here, da_s[...], jnp.zeros((), BF16))
        c = jnp.sum(jnp.where(lane == h, near_c, 0.0), axis=1, keepdims=True)
        dl = jnp.sum(jnp.where(lane == h, delta, 0.0), axis=1, keepdims=True)
        prob = exps[h] * c
        ds = (prob * (dprobs[h] - dl)).astype(BF16)
        qgrad[...] += jnp.where(here, dot(ds, keys), 0.0)
        kgrad[...] += dot_tn(ds, qh)
        vgrad[...] += dot_tn(prob.astype(BF16), dah)
        return _

    lax.fori_loop(0, heads, near_back, 0)
    for s, lo in ((0, 0), (1, 2 * nodes)):
        rim_out[s, :, :cw] = (kgrad[lo : lo + nodes, :] * scale).astype(BF16)
        rim_out[s, :, cw:] = vgrad[lo : lo + nodes, :].astype(BF16)

    @pl.when(me > 0)
    def _():
        rim_back(True).start()

    @pl.when(me < n - 1)
    def _():
        rim_back(False).start()

    half = outer // 2
    for mine in (True, False):
        block = dot_tn(g_ref[...] if mine else g_oth[...], att)
        first = (hd if mine else 1 - hd) * half
        if drows % 16:
            wide[0, :, :cw] = block
            for i in range(half * inner):
                dw_out[i % inner, pl.ds(first + i // inner, 1)] = (
                    wide[0, i * drows : (i + 1) * drows, :cw].astype(BF16)[None]
                )
        else:
            cut = block.astype(BF16).reshape(half, inner, drows, cw)
            for j in range(inner):
                dw_out[j, pl.ds(first, half)] = cut[:, j]
    every(lambda j: dw_copy(j, my_in).start(), my_in, inner)
    dw_in[pl.ds(my_in, 1)] = dw_out[pl.ds(my_in, 1)]

    qg_ref[...] = (qgrad[...] * scale).astype(BF16)
    send_w.wait_recv()
    send_att.wait_recv()
    lo_ref[...] = (dot(att, w_ref[:, my_cols]) + dot(att_oth[...], w_oth[...])).astype(BF16)

    every(lambda s: dw_copy(s, s).wait_recv(), my_in, inner)
    dw2_out[...] = jnp.sum(dw_in[...].astype(F32), axis=0).astype(BF16)
    every(lambda o: dw2_copy(o, my_out).start(), my_out, outer)
    dw2_in[pl.ds(my_out, 1)] = dw2_out[pl.ds(my_out, 1)]

    @pl.when(me > 0)
    def _():
        rim_back(False).wait_recv()

    @pl.when(me < n - 1)
    def _():
        rim_back(True).wait_recv()

    every(lambda s: dw2_copy(s, s).wait_recv(), my_out, outer)
    dw_ref[...] = jnp.sum(dw2_in[...].astype(F32), axis=0)
    every(lambda s: back_copy(s, s).wait_recv())
    own = dot(rows_t[...], flat_of(back_in[...]))
    rim = rim_in[0].astype(F32) + rim_in[1].astype(F32)
    own_k = kgrad[nodes : 2 * nodes, :] * scale
    kg_ref[...] = (own[:, :cw] + rim[:, :cw] + own_k).astype(BF16)
    vg_ref[...] = (own[:, cw:] + rim[:, cw:] + vgrad[nodes : 2 * nodes, :]).astype(BF16)

    def left(d):
        far_copy(d, me).wait_send()
        back_copy(d, me).wait_send()

    every(left)
    every(lambda j: dw_copy(j, my_in).wait_send(), my_in, inner)
    every(lambda o: dw2_copy(o, my_out).wait_send(), my_out, outer)
    send_g.wait_send()
    send_w.wait_send()
    send_att.wait_send()

    @pl.when(me > 0)
    def _():
        for c in rim_copies(True):
            c.wait_send()
        rim_back(True).wait_send()

    @pl.when(me < n - 1)
    def _():
        for c in rim_copies(False):
            c.wait_send()
        rim_back(False).wait_send()


def place(*refs):
    for i in range(5):
        refs[5 + i][...] = refs[i][...]


def shards(
    n, q, k, v, out_weight, out_grad, far_bias, tile_list, tile_count, send_rows, expander_slot
):
    nodes, cw = q.shape
    heads = far_bias.shape[0]
    cap = send_rows.shape[2]
    deg = expander_slot.shape[1]
    drows = 2 * cw // n
    inner = math.gcd(n, 4)
    ext = 3 * nodes
    slots = n * cap
    dma = pltpu.SemaphoreType.DMA
    vm = pl.BlockSpec(memory_space=pltpu.VMEM)
    sm = pl.BlockSpec(memory_space=pltpu.SMEM)
    node_out = jax.ShapeDtypeStruct((nodes, cw), BF16)
    anywhere = pl.BlockSpec(memory_space=pl.ANY)
    outs = pl.pallas_call(
        functools.partial(body, n),
        out_shape=(node_out, node_out, node_out, node_out, jax.ShapeDtypeStruct((drows, cw), F32)),
        in_specs=[anywhere] * 5 + [sm] * 3 + [vm] * 2,
        out_specs=(vm, vm, vm, vm, vm),
        scratch_shapes=[
            pltpu.VMEM((nodes, cw), BF16),
            pltpu.VMEM((cw, 2 * cw), BF16),
            pltpu.VMEM((nodes, cw), BF16),
            pltpu.VMEM((128, 128), jnp.int32),
            pltpu.VMEM((deg, nodes, slots), BF16),
            pltpu.VMEM((3, nodes, cw), BF16),
            pltpu.VMEM((3, nodes, cw), BF16),
            pltpu.VMEM((n, cap, 2 * cw), BF16),
            pltpu.VMEM((n, cap, 2 * cw), BF16),
            pltpu.VMEM((n, cap, 2 * cw), BF16),
            pltpu.VMEM((n, cap, 2 * cw), BF16),
            pltpu.VMEM((nodes, cw), BF16),
            pltpu.VMEM((cw, cw), BF16),
            pltpu.VMEM((nodes, cw), BF16),
            pltpu.VMEM((nodes, cw), BF16),
            pltpu.VMEM((2, nodes, 2 * cw), BF16),
            pltpu.VMEM((2, nodes, 2 * cw), BF16),
            pltpu.VMEM((inner, n // inner, drows, cw), BF16),
            pltpu.VMEM((inner, n // inner, drows, cw), BF16),
            pltpu.VMEM((n // inner, drows, cw), BF16),
            pltpu.VMEM((n // inner, drows, cw), BF16),
            pltpu.VMEM((heads, nodes, ext), F32),
            pltpu.VMEM((heads, nodes, ext), F32),
            pltpu.VMEM((deg * nodes, 2 * cw), BF16),
            pltpu.VMEM((nodes, ext), F32),
            pltpu.VMEM((nodes, cw), F32),
            pltpu.VMEM((nodes, 128), F32),
            pltpu.VMEM((nodes, 128), F32),
            pltpu.VMEM((ext, cw), F32),
            pltpu.VMEM((ext, cw), F32),
            pltpu.VMEM((nodes, cw), F32),
            pltpu.VMEM((slots, deg * nodes), BF16),
            pltpu.VMEM((nodes, slots), BF16),
            pltpu.VMEM((nodes, cw), BF16),
            pltpu.VMEM((deg, nodes, 2 * cw), F32),
            dma((n,)), dma((n,)), dma((4,)), dma((4,)), dma((n,)), dma((n,)),
            dma((2,)), dma((2,)), dma((inner,)), dma((inner,)), dma((n // inner,)), dma((n // inner,)),
            dma((3,)), dma((3,)), dma((5,)),
        ],
        compiler_params=pltpu.CompilerParams(
            collective_id=0, has_side_effects=True, vmem_limit_bytes=60 * 1024 * 1024
        ),
        name="exphormer",
    )(
        q, k, v, out_weight, out_grad, far_bias, tile_list, tile_count,
        send_rows, expander_slot.T,
    )
    return pl.pallas_call(
        place,
        out_shape=tuple(jax.ShapeDtypeStruct(o.shape, o.dtype) for o in outs),
        in_specs=[vm] * 5,
        out_specs=(vm,) * 5,
        name="place",
    )(*outs)


def solution(mesh):
    in_specs = (
        P("dom", "head"),
        P("dom", "head"),
        P("dom", "head"),
        P("head", None),
        P("dom", "head"),
        P("head"),
        P("dom", None),
        P("dom"),
        P("dom", None, None),
        P("dom", None),
    )
    out_specs = (P("dom", "head"),) * 5
    return jax.shard_map(
        functools.partial(shards, mesh.shape["dom"]),
        mesh=mesh, in_specs=in_specs, out_specs=out_specs, check_vma=False,
    )
```
